32 devices in a mesh: dp: 8 (over z, x), ctx: 4 (over y, core).
Axes of the slice: x: 2, y: 2, z: 4, core: 2. Of those that a mesh axis runs over, the one named last changes fastest.
Arguments:
- tokens: bfloat16 [16, 256, 1024], P('dp', 'ctx'), may hold values from -6 to 6
- segments: int32 [16, 256], P('dp', 'ctx'), may hold values from 0 to 15, as said below
- norm_gain: bfloat16 [1024], P(('dp', 'ctx')), may hold values from 0.099609375 to 1.8984375
- in_weight: bfloat16 [1024, 3072], P(('dp', 'ctx')), may hold values from -0.1875 to 0.1875
- conv_taps: bfloat16 [3, 1024], P(None, ('dp', 'ctx')), may hold values from -3 to 3
- out_weight: bfloat16 [1024, 1024], P(('dp', 'ctx')), may hold values from -0.1875 to 0.1875
- ffn_gain: bfloat16 [1024], P(('dp', 'ctx')), may hold values from 0.099609375 to 1.8984375
- gate_weight: bfloat16 [1024, 4608], P(('dp', 'ctx')), may hold values from -0.1875 to 0.1875
- up_weight: bfloat16 [1024, 4608], P(('dp', 'ctx')), may hold values from -0.1875 to 0.1875
- down_weight: bfloat16 [4608, 1024], P(('dp', 'ctx')), may hold values from -0.09375 to 0.09375
- cotangent: bfloat16 [16, 256, 1024], P('dp', 'ctx'), may hold values from -6 to 6
Outputs:
- mixed: bfloat16 [16, 256, 1024], P('dp', 'ctx')
- input_grad: float32 [16, 256, 1024], P('dp', 'ctx')
- grad_norm_gain: float32 [1024], P(('dp', 'ctx'))
- grad_in_weight: float32 [1024, 3072], P(('dp', 'ctx'))
- grad_conv_taps: float32 [3, 1024], P(None, ('dp', 'ctx'))
- grad_out_weight: float32 [1024, 1024], P(('dp', 'ctx'))
- grad_ffn_gain: float32 [1024], P(('dp', 'ctx'))
- grad_gate_weight: float32 [1024, 4608], P(('dp', 'ctx'))
- grad_up_weight: float32 [1024, 4608], P(('dp', 'ctx'))
- grad_down_weight: float32 [4608, 1024], P(('dp', 'ctx'))
The draws below stay inside these ranges and needn't reach their ends.
Inputs may be any that keep to these rules, and one draw needn't show every extreme that they name: `segments`: within each sequence the numbers start at 0 at its first position and rise by one at the first position of each new document. Among the 2 sequences of one index of dp, one drawn from the seed holds a single document; every other sequence holds exactly 16 documents.
All inputs are finite; a program needn't handle non-finite values.
Results may differ from the reference program's by a relative error of at most 0.0092.
Values may be sent and summed in bfloat16 or wider, within the bound.
No kernel may reach another device: no remote copies, remote signals or barrier semaphores. Data moves between devices by JAX's collectives and lax.ppermute only.
A program may use at most 320 MiB of HBM per device.

```python
import math
import jax
import jax.numpy as jnp
from jax import lax

D = 1024
FF = 4608
TAPS = 3
MB = 2
LENGTH = 256
BATCH = 16


def draw_segments(key, part):
    key = jax.random.fold_in(key, 11)
    score_key = jax.random.fold_in(key, 1)
    pick_key = jax.random.fold_in(key, 2)
    bound_count = max(1, LENGTH // 16 - 1)
    position = lax.broadcasted_iota(jnp.int32, (BATCH, LENGTH), 1)
    raw_scores = jax.random.randint(score_key, (BATCH, LENGTH), 0, LENGTH).astype(jnp.int32)
    score_values = jnp.where(position > 0, raw_scores * LENGTH + position, -1).astype(jnp.int32)
    picked = lax.top_k(score_values, bound_count)[1].astype(jnp.int32)
    starts = jnp.any(position[:, :, None] == picked[:, None, :], axis=2)
    groups = BATCH // MB
    chosen = jax.random.randint(pick_key, (groups,), 0, MB)
    member = (lax.broadcasted_iota(jnp.int32, (groups, MB), 1) == chosen[:, None]).reshape(BATCH, 1)
    starts = starts & jnp.logical_not(member)
    return jnp.cumsum(starts.astype(jnp.int32), axis=1).astype(jnp.int32)


def raised(result, key, source, target, shards_of, factor):
    def block_of(dim):
        return (jnp.arange(result.shape[dim]) // (result.shape[dim] // shards_of)).reshape((-1,) + (1,) * (result.ndim - 1 - dim))

    first = jax.random.permutation(key, shards_of)[block_of(target)]
    second = (block_of(target) + shards_of // 2) % shards_of
    return jnp.where((block_of(source) == first) | (block_of(source) == second), factor * result, result)


def steps_of(rng, dims, split, smallest, top_value):
    level, own = 1.0, jax.random.fold_in(rng, 6)
    for axis_at, shards_of in split:
        heights = jnp.exp(jax.random.uniform(jax.random.fold_in(own, axis_at), (shards_of,), jnp.float32, smallest / len(split), top_value / len(split)))
        level = level * jnp.repeat(heights, dims[axis_at] // shards_of).reshape([-1 if axis == axis_at else 1 for axis in range(len(dims))])
    return level


def scatter_about(rng, dims, width, reach, split=(), dtype=jnp.bfloat16):
    drawn = jax.random.normal(rng, dims, jnp.float32) * width
    if len(split) > 0:
        drawn = steps_of(rng, dims, split, -0.22, 0.18) * drawn
    return jnp.clip(drawn, min=-reach, max=reach).astype(dtype)


def heavy_noise(rng, extent, width, reach, shards, heavy, held_as=jnp.bfloat16):
    values = width * jax.random.normal(rng, extent, jnp.float32)
    if shards:
        values = values * steps_of(rng, extent, shards, -0.22, 0.18)
    return jnp.clip(raised(values, jax.random.fold_in(rng, 3), *heavy), -reach, reach).astype(held_as)


def setup_inputs(seed: int = 0) -> dict:
    key_of = jax.random.split(jax.random.key(seed), 12)
    return {
        "tokens": heavy_noise(key_of[0], (BATCH, LENGTH, D), 1.0, 6.0, ((0, 8), (1, 4)), (0, 2, 8, 2.0)),
        "segments": draw_segments(jax.random.fold_in(key_of[11], 71), 0),
        "norm_gain": jnp.clip(1.0 + 0.18 * jax.random.normal(key_of[2], (D,), jnp.float32), 0.099609375, 1.8984375).astype(jnp.bfloat16),
        "in_weight": scatter_about(key_of[3], (D, 3 * D), D ** -0.5, 0.1875, ((0, 32),)),
        "conv_taps": scatter_about(key_of[4], (TAPS, D), 0.6, 3.0, ((1, 32),)),
        "out_weight": scatter_about(key_of[5], (D, D), D ** -0.5, 0.1875, ((0, 32),)),
        "ffn_gain": jnp.clip(1.0 + 0.18 * jax.random.normal(key_of[6], (D,), jnp.float32), 0.099609375, 1.8984375).astype(jnp.bfloat16),
        "gate_weight": scatter_about(key_of[7], (D, FF), D ** -0.5, 0.1875, ((0, 32),)),
        "up_weight": scatter_about(key_of[8], (D, FF), D ** -0.5, 0.1875, ((0, 32),)),
        "down_weight": scatter_about(key_of[9], (FF, D), FF ** -0.5, 0.09375, ((0, 32),)),
        "cotangent": scatter_about(key_of[10], (BATCH, LENGTH, D), 1.0, 6.0, ((0, 8), (1, 4))),
    }


EPS = 1e-05

@jax.custom_vjp
def low(v):
    return lax.optimization_barrier(v.astype(jnp.bfloat16)).astype(jnp.float32)

@jax.custom_vjp
def low_back(v):
    return v

def low_keep(v):
    return (low(v), None)

def low_pass(kept, grad):
    return (grad,)

def back_keep(v):
    return (v, None)

def back_low(kept, grad):
    return (low(grad),)
low.defvjp(low_keep, low_pass)
low_back.defvjp(back_keep, back_low)

def normalize_rows(values, gain):
    return values * lax.rsqrt(lax.optimization_barrier(jnp.mean(values * values, axis=-1, keepdims=True)) + EPS) * gain

def product(left_operand, right_operand):
    return jnp.einsum('zma,ak->zmk', left_operand, right_operand, precision=lax.Precision.HIGHEST)

def short_conv(mixed_in, tap_values, documents):
    keep_one = jnp.concatenate([jnp.zeros_like(documents[:, :1]), (documents[:, 1:] == documents[:, :-1]).astype(jnp.int32)], axis=1)
    keep_two = jnp.concatenate([jnp.zeros_like(documents[:, :2]), (documents[:, 2:] == documents[:, :-2]).astype(jnp.int32)], axis=1)
    blank_one = jnp.zeros_like(mixed_in[:, :1])
    empty_second = jnp.zeros_like(mixed_in[:, :2])
    previous = jnp.concatenate([blank_one, mixed_in[:, :-1]], axis=1)
    earlier = jnp.concatenate([empty_second, mixed_in[:, :-2]], axis=1)
    mask_one = keep_one.astype(jnp.float32)[:, :, None]
    mask_two = keep_two.astype(jnp.float32)[:, :, None]
    return tap_values[2] * mixed_in + tap_values[1] * previous * mask_one + tap_values[0] * earlier * mask_two

def block_forward(inputs, documents, params):
    gain_one, weight_in, tap_values, weight_out, gain_two, weight_gate, weight_up, weight_down = params
    hidden_in = low(normalize_rows(inputs, gain_one))
    projected = low_back(product(hidden_in, weight_in))
    part_b = projected[..., :D]
    part_c = projected[..., D:2 * D]
    part_x = projected[..., 2 * D:]
    mixed_in = low(part_b * part_x)
    shortconv = low_back(short_conv(mixed_in, tap_values, documents))
    gated = low(part_c * shortconv)
    branch_path = low_back(product(gated, weight_out))
    resid = inputs + branch_path
    hidden_ffn = low(normalize_rows(resid, gain_two))
    gate_act = low_back(product(hidden_ffn, weight_gate))
    upward = low_back(product(hidden_ffn, weight_up))
    hidden = low(jax.nn.silu(gate_act) * upward)
    return resid + product(hidden, weight_down)

def reference(tokens, segments, norm_gain, in_weight, conv_taps, out_weight, ffn_gain, gate_weight, up_weight, down_weight, cotangent):
    group_size = math.gcd(BATCH, max(1, 4096 // LENGTH))
    step_count = BATCH // group_size
    weights = (norm_gain.astype(jnp.float32), in_weight.astype(jnp.float32), conv_taps.astype(jnp.float32), out_weight.astype(jnp.float32), ffn_gain.astype(jnp.float32), gate_weight.astype(jnp.float32), up_weight.astype(jnp.float32), down_weight.astype(jnp.float32))

    def by_group(values):
        return values.reshape((step_count, group_size) + values.shape[1:])

    def one_group(running, block_data):
        token_rows, documents, seed_rows = block_data

        def forward(inputs, *params):
            return block_forward(inputs, documents, params)
        result_rows, pullback = jax.vjp(forward, token_rows.astype(jnp.float32), *weights)
        gradients = pullback(seed_rows.astype(jnp.float32))
        running = tuple((before + after for before, after in zip(running, gradients[1:])))
        return (running, (result_rows.astype(jnp.bfloat16), gradients[0]))
    starting = tuple((jnp.zeros(weight_item.shape, jnp.float32) for weight_item in weights))
    totals, (mixed, input_grad) = lax.scan(one_group, starting, (by_group(tokens), by_group(segments), by_group(cotangent)))
    mixed = mixed.reshape(BATCH, LENGTH, D)
    input_grad = input_grad.reshape(BATCH, LENGTH, D)
    return (mixed, input_grad, totals[0], totals[1], totals[2], totals[3], totals[4], totals[5], totals[6], totals[7])
```

```python
import functools

import jax
import jax.numpy as jnp
from jax import lax
from jax.experimental import pallas as pl
from jax.experimental.pallas import tpu as pltpu
from jax.sharding import Mesh
from jax.sharding import PartitionSpec as P

EPS = 1e-05
PLANE = ("near", "ctx")


def mate(value, flip):
    count = lax.axis_size("near") * lax.axis_size("ctx")
    return lax.ppermute(value, PLANE, [(k, k ^ flip) for k in range(count)])


def from_planes(block):
    count = lax.axis_size("far")
    came = [block] + [
        lax.ppermute(block, "far", [(f, (f + s) % count) for f in range(count)])
        for s in range(1, count)
    ]
    came = came[::-1]
    start = lax.rem(2 * count - 1 - lax.axis_index("far"), count) * block.shape[0]
    twice = jnp.concatenate(came + came)
    return lax.dynamic_slice_in_dim(twice, start, count * block.shape[0], axis=0)


def reach(block):
    count = lax.axis_size("near") * lax.axis_size("ctx")
    return [block] + [mate(block, flip) for flip in range(2, count, 2)]


def collect(block):
    same = reach(block)
    return same + [mate(b, 1) for b in same]


def halves(blocks):
    half = len(blocks) // 2
    return jnp.concatenate(blocks[:half]), jnp.concatenate(blocks[half:])


def ffn_rows(steps, count, *refs):
    n2_blocks, seed_blocks = refs[:count], refs[count : 2 * count]
    gate_w, up_w, down_w, n2, seed, hid, dgate, dup, mix, same, other = refs[2 * count :]
    f32, bf = jnp.float32, jnp.bfloat16
    rows = n2_blocks[0].shape[0]
    for k in range(count):

        @pl.when(pl.program_id(0) == k * steps // count)
        def _():
            at = k % (count // steps) * rows
            n2[at : at + rows, :] = n2_blocks[k][...]
            seed[at : at + rows, :] = seed_blocks[k][...]

    x = n2[...]
    gate = jnp.dot(x, gate_w[...], preferred_element_type=f32)
    up = jnp.dot(x, up_w[...], preferred_element_type=f32)
    sig = 1.0 / (1.0 + jnp.exp(-gate))
    swish = gate * sig
    h = (swish * up).astype(bf)
    hid[...] = h
    mix[...] = jnp.dot(h, down_w[...], preferred_element_type=f32).astype(bf)
    d_hidden = against(seed[...], down_w[...])
    dg = (d_hidden * up * sig * (1.0 + gate * (1.0 - sig))).astype(bf)
    du = (d_hidden * swish).astype(bf)
    dgate[...] = dg
    dup[...] = du
    d_n2 = against(dg, gate_w[...]) + against(du, up_w[...])
    half = pl.num_programs(0) // 2

    @pl.when(pl.program_id(0) < half)
    def _():
        same[...] = d_n2

    @pl.when(pl.program_id(0) >= half)
    def _():
        other[...] = d_n2.astype(bf)


def ffn(n2_blocks, seed_blocks, w_gate, w_up, w_down):
    count = len(n2_blocks)
    block, features = n2_blocks[0].shape
    rows = count * block
    part = w_gate.shape[1]
    steps = 4
    tile = rows // steps
    f32, bf = jnp.float32, jnp.bfloat16
    row = lambda width: pl.BlockSpec((tile, width), lambda i: (i, 0))
    whole = lambda w: pl.BlockSpec(w.shape, lambda i: (0, 0))
    operands = (*n2_blocks, *seed_blocks, w_gate, w_up, w_down)
    widths = [features, features, part, part, part, features]
    return pl.pallas_call(
        functools.partial(ffn_rows, steps, count),
        grid=(steps,),
        in_specs=[whole(w) for w in operands],
        out_specs=[row(width) for width in widths]
        + [
            pl.BlockSpec((tile, features), lambda i: (jnp.minimum(i, steps // 2 - 1), 0)),
            pl.BlockSpec((tile, features), lambda i: (jnp.maximum(i - steps // 2, 0), 0)),
        ],
        out_shape=[jax.ShapeDtypeStruct((rows, width), bf) for width in widths]
        + [
            jax.ShapeDtypeStruct((rows // 2, features), f32),
            jax.ShapeDtypeStruct((rows // 2, features), bf),
        ],
        compiler_params=pltpu.CompilerParams(vmem_limit_bytes=48 * 2**20),
        cost_estimate=pl.CostEstimate(
            flops=12 * rows * features * part,
            bytes_accessed=6 * features * part + 14 * rows * features + 6 * rows * part,
            transcendentals=rows * part,
        ),
        name="ffn_rows",
    )(*operands)


def ffn_sums(n2, seed, hid, dgate, dup, g_gate, g_up, g_down, turned):
    @pl.when(pl.program_id(0) == 0)
    def _():
        turned[...] = hid[...].T

    bf = jnp.bfloat16
    g_gate[...] = across(n2[...], dgate[...]).astype(bf)
    g_up[...] = across(n2[...], dup[...]).astype(bf)
    g_down[...] = dot(turned[...], seed[...]).astype(bf)


def weight_sums(n2, seed, hid, dgate, dup):
    rows, features = n2.shape
    part = hid.shape[1]
    tile = features // 4
    bf = jnp.bfloat16
    column = lambda height: pl.BlockSpec((height, tile), lambda i: (0, i))
    whole = pl.BlockSpec((rows, part), lambda i: (0, 0))
    return pl.pallas_call(
        ffn_sums,
        grid=(4,),
        in_specs=[column(rows), column(rows), whole, whole, whole],
        out_specs=[
            pl.BlockSpec((tile, part), lambda i: (i, 0)),
            pl.BlockSpec((tile, part), lambda i: (i, 0)),
            column(part),
        ],
        out_shape=[
            jax.ShapeDtypeStruct((features, part), bf),
            jax.ShapeDtypeStruct((features, part), bf),
            jax.ShapeDtypeStruct((part, features), bf),
        ],
        scratch_shapes=[pltpu.VMEM((part, rows), bf)],
        compiler_params=pltpu.CompilerParams(vmem_limit_bytes=48 * 2**20),
        cost_estimate=pl.CostEstimate(
            flops=6 * rows * features * part,
            bytes_accessed=4 * rows * features + 6 * rows * part + 6 * features * part,
            transcendentals=0,
        ),
        name="ffn_sums",
    )(n2, seed, hid, dgate, dup)


def reduce_rows(same, other, beside=(), after=()):
    count = lax.axis_size("near") * lax.axis_size("ctx")
    arrived = mate(other.astype(jnp.bfloat16), 1)
    arrived, *after = lax.optimization_barrier((arrived, *after))
    total = same + arrived.astype(jnp.float32)
    blocks = total.reshape(count // 2, -1, total.shape[-1])
    sent = blocks.astype(jnp.bfloat16)
    result, *beside = lax.optimization_barrier((blocks[0], *beside))
    for k in range(1, count // 2):
        result = result + mate(sent[k], 2 * k).astype(jnp.float32)
    return (result, *beside, *after) if beside or after else result


def flipped(values):
    me = lax.axis_index("ctx")
    count = lax.axis_size("ctx")
    bit = 1
    while bit < count:
        v = values.reshape(values.shape[0], count // (2 * bit), 2, bit, *values.shape[2:])
        swapped = jnp.concatenate([v[:, :, 1:], v[:, :, :1]], axis=2)
        values = jnp.where((me & bit) != 0, swapped, v).reshape(values.shape)
        bit *= 2
    return values


def in_order(blocks):
    count = blocks.shape[0]
    me = lax.axis_index("near") * lax.axis_size("ctx") + lax.axis_index("ctx")
    bit = 1
    while bit < count:
        v = blocks.reshape(count // (2 * bit), 2, bit, *blocks.shape[1:])
        swapped = jnp.concatenate([v[:, 1:], v[:, :1]], axis=1)
        blocks = jnp.where((me & bit) != 0, swapped, v).reshape(blocks.shape)
        bit *= 2
    return blocks


def dot(a, b):
    return jnp.dot(a, b, preferred_element_type=jnp.float32)


def across(a, b):
    return lax.dot_general(a, b, (((0,), (0,)), ((), ())), preferred_element_type=jnp.float32)


def against(a, b):
    return lax.dot_general(a, b, (((1,), (1,)), ((), ())), preferred_element_type=jnp.float32)


def scale_rows(values):
    return lax.rsqrt(jnp.mean(values * values, axis=-1, keepdims=True) + EPS)


def norm_back(grad_normed, normed, inverse):
    return inverse * (grad_normed - normed * jnp.mean(grad_normed * normed, axis=-1, keepdims=True))


def on_device(
    tokens,
    segments,
    norm_gain,
    in_weight,
    conv_taps,
    out_weight,
    ffn_gain,
    gate_weight,
    up_weight,
    down_weight,
    cotangent,
):
    seq_count, seq_rows, features = tokens.shape
    rows = seq_count * seq_rows
    n_far = lax.axis_size("far")
    n_near = lax.axis_size("near")
    n_ctx = lax.axis_size("ctx")
    members = n_near * n_ctx
    own = in_weight.shape[0]
    own_ff = down_weight.shape[0]
    part = features // members
    part_ff = n_far * own_ff
    bf, f32 = jnp.bfloat16, jnp.float32
    gain_two = ffn_gain.astype(f32)[:, None]

    everyone = ("far",) + PLANE
    total = n_far * members
    own_tokens = tokens.reshape(rows, features)
    seed_rows = cotangent.reshape(rows, features)

    small = jnp.zeros((16, 128), bf)
    small = small.at[0, :own].set(norm_gain)
    small = small.at[8 : 8 + rows // 128, :].set(segments.reshape(rows // 128, 128).astype(bf))
    small = jnp.broadcast_to(small[None], (total, 16, 128))
    small = lax.all_to_all(small, everyone, split_axis=0, concat_axis=0, tiled=True)
    gain_row = small[:, 0, :own].reshape(features).astype(f32)
    seg_all = lax.dynamic_slice_in_dim(small, lax.axis_index("far") * members, members, axis=0)
    seg_all = seg_all[:, 8 : 8 + rows // 128].reshape(members, rows)
    in_cut = in_weight.reshape(own, 3, total, own).transpose(2, 0, 1, 3)
    in_cut = in_cut.reshape(n_far, members, own, 3, own).transpose(1, 2, 3, 0, 4)
    in_cut = in_cut.reshape(1, members, own, 3 * part)
    in_cut = jnp.broadcast_to(in_cut, (n_far, members, own, 3 * part))
    in_cut = in_cut.reshape(total, own, 3 * part)
    in_cut = lax.all_to_all(in_cut, everyone, split_axis=0, concat_axis=0, tiled=True)
    w_in = in_cut.reshape(features, 3 * part)
    tap_rows = jnp.pad(conv_taps, ((0, 13), (0, features - own)))
    lower = jnp.concatenate([down_weight, out_weight, tap_rows], axis=0)
    lower = lax.all_gather(lower, "far", axis=0, tiled=False)
    w_down = lower[:, :own_ff].reshape(part_ff, features)
    w_out = lower[:, own_ff : own_ff + own].reshape(part, features)
    taps = lower[:, own_ff + own : own_ff + own + 3, :own].astype(f32)
    taps = taps.transpose(1, 0, 2).reshape(3, part)

    def cut_ff(weight):
        scaled = (weight.astype(f32) * gain_two).astype(bf)
        cut = scaled.reshape(own, n_far, members, own_ff).transpose(2, 0, 1, 3)
        return cut.reshape(members, own, part_ff)

    gu_cut = jnp.stack([cut_ff(gate_weight), cut_ff(up_weight)], axis=1)
    gu_cut = lax.all_to_all(gu_cut, PLANE, split_axis=0, concat_axis=0, tiled=True)
    gu_rows = gu_cut.transpose(1, 0, 2, 3).reshape(2, members * own, part_ff)
    gu_all = lax.all_gather(gu_rows, "far", axis=0, tiled=False)
    w_gate = gu_all[:, 0].reshape(features, part_ff)
    w_up = gu_all[:, 1].reshape(features, part_ff)

    seg_true = seg_all.reshape(n_near, n_ctx, seq_count, seq_rows).transpose(0, 2, 1, 3)
    me_near = lax.axis_index("near")
    seg_true = jnp.where(me_near == 0, seg_true, seg_true[::-1])
    length = n_ctx * seq_rows
    seg_true = seg_true.reshape(n_near * seq_count, length)
    outside = jnp.full((n_near * seq_count, 2), -1, bf)
    seg_ext = jnp.concatenate([outside, seg_true], axis=1)
    keep1 = (seg_ext[:, 1 : length + 1] == seg_true).astype(f32)[:, :, None]
    keep2 = (seg_ext[:, :length] == seg_true).astype(f32)[:, :, None]

    def to_true(same, other):
        v = jnp.stack(
            [
                same.reshape(n_near, n_ctx // 2, seq_count, seq_rows, -1),
                other.reshape(n_near, n_ctx // 2, seq_count, seq_rows, -1),
            ],
            axis=2,
        )
        v = flipped(v.reshape(n_near, n_ctx, seq_count, seq_rows, -1))
        return v.transpose(0, 2, 1, 3, 4).reshape(n_near * seq_count, length, -1)

    def to_relative(v):
        v = v.reshape(n_near, seq_count, n_ctx, seq_rows, -1).transpose(0, 2, 1, 3, 4)
        v = flipped(v).reshape(n_near, n_ctx // 2, 2, seq_count, seq_rows, -1)
        half = members // 2 * rows
        return v[:, :, 0].reshape(half, -1), v[:, :, 1].reshape(half, -1)

    def shifted(v, steps):
        fill = jnp.zeros((v.shape[0], abs(steps), v.shape[2]), v.dtype)
        if steps > 0:
            return jnp.concatenate([fill, v[:, :-steps]], axis=1)
        return jnp.concatenate([v[:, -steps:], fill], axis=1)

    def normalized(t):
        v = t.astype(f32)
        return (v * scale_rows(v) * gain_row).astype(bf)

    def summed(left, right):
        return across(left[0], right[0]) + across(left[1], right[1])

    x_all = collect(own_tokens)
    x_all, seed_rows = lax.optimization_barrier((x_all, seed_rows))
    seed_all = collect(seed_rows)
    w_in, seed_all = lax.optimization_barrier((w_in, seed_all))
    x_all = halves(x_all)
    h_in = tuple(normalized(t) for t in x_all)
    proj = [dot(n, w_in) for n in h_in]
    part_b = [p[:, :part] for p in proj]
    part_c = [p[:, part : 2 * part] for p in proj]
    part_x = [p[:, 2 * part :] for p in proj]
    mixed_in = to_true(*[(b * x).astype(bf) for b, x in zip(part_b, part_x)]).astype(f32)
    previous = shifted(mixed_in, 1) * keep1
    earlier = shifted(mixed_in, 2) * keep2
    short = to_relative(taps[2] * mixed_in + taps[1] * previous + taps[0] * earlier)
    gated = [(c * s).astype(bf) for c, s in zip(part_c, short)]
    branch = reduce_rows(*[dot(g, w_out) for g in gated])
    resid = own_tokens.astype(f32) + branch
    inverse2 = scale_rows(resid)
    normed2 = resid * inverse2

    n2_all = collect(normed2.astype(bf))
    n2_all, seed_all, hidden, d_gate, d_up, part_mixed, d_same, d_other = ffn(
        n2_all, seed_all, w_gate, w_up, w_down
    )
    sum_gate, sum_up, sum_down = weight_sums(n2_all, seed_all, hidden, d_gate, d_up)
    sum_down = sum_down.reshape(n_far, own_ff, features)
    d_n2, sum_gate, sum_up, sum_down = reduce_rows(
        d_same, d_other, beside=(sum_gate, sum_up, sum_down)
    )
    own_gu = jnp.stack(
        [
            lax.psum_scatter(sum_gate, "far", scatter_dimension=0, tiled=True),
            lax.psum_scatter(sum_up, "far", scatter_dimension=0, tiled=True),
        ]
    )
    d_resid = seed_rows.astype(f32) + norm_back(d_n2, normed2, inverse2)

    d_branch = collect(d_resid.astype(bf))
    d_branch = halves(d_branch)
    d_branch, part_mixed = lax.optimization_barrier((d_branch, part_mixed))
    mixed = (resid + reduce_rows(*[m.astype(f32) for m in jnp.split(part_mixed, 2)])).astype(bf)
    d_gated = [against(d, w_out) for d in d_branch]
    d_short = to_true(*[(d * c).astype(bf) for d, c in zip(d_gated, part_c)]).astype(f32)
    sum_taps = jnp.stack(
        [
            jnp.sum(d_short * earlier, axis=(0, 1)),
            jnp.sum(d_short * previous, axis=(0, 1)),
            jnp.sum(d_short * mixed_in, axis=(0, 1)),
        ]
    )
    d_mixed = to_relative(
        taps[2] * d_short
        + shifted(taps[1] * keep1 * d_short, -1)
        + shifted(taps[0] * keep2 * d_short, -2)
    )
    d_proj = [
        jnp.concatenate([dm * x, dg * s, dm * b], axis=1).astype(bf)
        for dm, dg, s, b, x in zip(d_mixed, d_gated, short, part_b, part_x)
    ]
    sum_in = summed(h_in, d_proj).astype(bf).reshape(total, own, 3 * part)
    d_proj, sum_in = lax.optimization_barrier((d_proj, sum_in))
    d_n1 = reduce_rows(*[against(d, w_in) for d in d_proj]) * gain_row
    values = own_tokens.astype(f32)
    inverse1 = scale_rows(values)
    input_grad = d_resid + norm_back(d_n1, values * inverse1, inverse1)

    own_in = lax.all_to_all(sum_in, everyone, split_axis=0, concat_axis=0, tiled=True)
    own_in = own_in.reshape(n_far, members, own, 3 * part).astype(f32).sum(axis=0)
    own_in = own_in.reshape(members, own, 3, n_far, own).transpose(1, 2, 3, 0, 4)
    grad_in = own_in.reshape(own, 3 * features)
    grad_gain1 = jnp.sum(in_weight.astype(f32) * grad_in, axis=1) / norm_gain.astype(f32)
    sum_out = summed(gated, d_branch).astype(bf).reshape(n_far, own, features)
    tap_sums = sum_taps.astype(bf).reshape(3, n_far, own).transpose(1, 0, 2)
    tap_sums = jnp.pad(tap_sums, ((0, 0), (0, 13), (0, features - own)))
    lower_sum = jnp.concatenate([sum_down, sum_out, tap_sums], axis=1)
    own_gu = own_gu.reshape(2, members, own, part_ff).transpose(1, 0, 2, 3)
    own_gu = lax.all_to_all(own_gu, PLANE, split_axis=0, concat_axis=0, tiled=True)
    own_lower = lax.psum_scatter(lower_sum, "far", scatter_dimension=0, tiled=False)
    own_lower = own_lower.astype(f32)
    grad_out = own_lower[own_ff : own_ff + own]
    grad_taps = own_lower[own_ff + own : own_ff + own + 3, :own]
    own_gu = own_gu.reshape(members, 2, own, n_far, own_ff).transpose(1, 2, 3, 0, 4)
    own_gu = own_gu.reshape(2, own, members * part_ff).astype(f32)
    grad_gate = own_gu[0] * gain_two
    grad_up = own_gu[1] * gain_two
    grad_gain2 = jnp.sum(
        gate_weight.astype(f32) * own_gu[0] + up_weight.astype(f32) * own_gu[1], axis=1
    )
    return (
        mixed.reshape(seq_count, seq_rows, features),
        input_grad.reshape(seq_count, seq_rows, features),
        grad_gain1,
        grad_in,
        grad_taps,
        grad_out,
        grad_gain2,
        grad_gate,
        grad_up,
        own_lower[:own_ff],
    )


def solution(mesh):
    dp, ctx = mesh.shape["dp"], mesh.shape["ctx"]
    near = 2 if dp % 2 == 0 else 1
    fine = Mesh(mesh.devices.reshape(dp // near, near, ctx), ("far", "near", "ctx"))
    seq = ("far", "near")
    every = ("far", "near", "ctx")
    in_specs = (
        P(seq, "ctx", None),
        P(seq, "ctx"),
        P(every),
        P(every, None),
        P(None, every),
        P(every, None),
        P(every),
        P(every, None),
        P(every, None),
        P(every, None),
        P(seq, "ctx", None),
    )
    out_specs = (
        P(seq, "ctx", None),
        P(seq, "ctx", None),
        P(every),
        P(every, None),
        P(None, every),
        P(every, None),
        P(every),
        P(every, None),
        P(every, None),
        P(every, None),
    )
    return jax.shard_map(
        on_device, mesh=fine, in_specs=in_specs, out_specs=out_specs, check_vma=False
    )
```

```python
import functools

import jax
import jax.numpy as jnp
from jax import lax
from jax.experimental import pallas as pl
from jax.experimental.pallas import tpu as pltpu
from jax.sharding import Mesh
from jax.sharding import PartitionSpec as P

EPS = 1e-05
PLANE = ("near", "ctx")


def mate(value, flip):
    count = lax.axis_size("near") * lax.axis_size("ctx")
    return lax.ppermute(value, PLANE, [(k, k ^ flip) for k in range(count)])


def from_planes(block):
    count = lax.axis_size("far")
    came = [block] + [
        lax.ppermute(block, "far", [(f, (f + s) % count) for f in range(count)])
        for s in range(1, count)
    ]
    came = came[::-1]
    start = lax.rem(2 * count - 1 - lax.axis_index("far"), count) * block.shape[0]
    twice = jnp.concatenate(came + came)
    return lax.dynamic_slice_in_dim(twice, start, count * block.shape[0], axis=0)


def reach(block):
    count = lax.axis_size("near") * lax.axis_size("ctx")
    return [block] + [mate(block, flip) for flip in range(2, count, 2)]


def collect(block):
    same = reach(block)
    return same + [mate(b, 1) for b in same]


def halves(blocks):
    half = len(blocks) // 2
    return jnp.concatenate(blocks[:half]), jnp.concatenate(blocks[half:])


def ffn_first(steps, count, *refs):
    n2_blocks, seed_blocks = refs[:count], refs[count : 2 * count]
    gate_w, down_w, n2, seed, gate, d_hidden = refs[2 * count :]
    rows = n2_blocks[0].shape[0]
    for k in range(count):

        @pl.when(pl.program_id(0) == k * steps // count)
        def _():
            at = k % (count // steps) * rows
            n2[at : at + rows, :] = n2_blocks[k][...]
            seed[at : at + rows, :] = seed_blocks[k][...]

    gate[...] = dot(n2[...], gate_w[...])
    d_hidden[...] = against(seed[...], down_w[...])


def ffn_rows(n2, gate_in, d_hidden_in, gate_w, up_w, hid, dgate, dup, same, other):
    bf = jnp.bfloat16
    up = dot(n2[...], up_w[...])
    gate = gate_in[...]
    d_hidden = d_hidden_in[...]
    sig = 1.0 / (1.0 + jnp.exp(-gate))
    swish = gate * sig
    hid[...] = (swish * up).astype(bf)
    dg = (d_hidden * up * sig * (1.0 + gate * (1.0 - sig))).astype(bf)
    du = (d_hidden * swish).astype(bf)
    dgate[...] = dg
    dup[...] = du
    d_n2 = against(dg, gate_w[...]) + against(du, up_w[...])
    half = pl.num_programs(0) // 2

    @pl.when(pl.program_id(0) < half)
    def _():
        same[...] = d_n2

    @pl.when(pl.program_id(0) >= half)
    def _():
        other[...] = d_n2.astype(bf)


def ffn(n2_blocks, seed_blocks, w_gate, w_up, w_down):
    count = len(n2_blocks)
    block, features = n2_blocks[0].shape
    rows = count * block
    part = w_gate.shape[1]
    steps = 4
    tile = rows // steps
    f32, bf = jnp.float32, jnp.bfloat16
    row = lambda width: pl.BlockSpec((tile, width), lambda i: (i, 0))
    whole = lambda w: pl.BlockSpec(w.shape, lambda i: (0, 0))
    shape = lambda width, kind: jax.ShapeDtypeStruct((rows, width), kind)
    params = pltpu.CompilerParams(vmem_limit_bytes=48 * 2**20)
    operands = (*n2_blocks, *seed_blocks, w_gate, w_down)
    n2, seed, gate, d_hidden = pl.pallas_call(
        functools.partial(ffn_first, steps, count),
        grid=(steps,),
        in_specs=[whole(w) for w in operands],
        out_specs=[row(features), row(features), row(part), row(part)],
        out_shape=[
            shape(features, bf),
            shape(features, bf),
            shape(part, f32),
            shape(part, f32),
        ],
        compiler_params=params,
        cost_estimate=pl.CostEstimate(
            flops=4 * rows * features * part,
            bytes_accessed=4 * features * part + 8 * rows * features + 8 * rows * part,
            transcendentals=0,
        ),
        name="ffn_first",
    )(*operands)
    hidden, d_gate, d_up, d_same, d_other = pl.pallas_call(
        ffn_rows,
        grid=(steps,),
        in_specs=[row(features), row(part), row(part), whole(w_gate), whole(w_up)],
        out_specs=[
            row(part),
            row(part),
            row(part),
            pl.BlockSpec((tile, features), lambda i: (jnp.minimum(i, steps // 2 - 1), 0)),
            pl.BlockSpec((tile, features), lambda i: (jnp.maximum(i - steps // 2, 0), 0)),
        ],
        out_shape=[shape(part, bf), shape(part, bf), shape(part, bf)]
        + [
            jax.ShapeDtypeStruct((rows // 2, features), f32),
            jax.ShapeDtypeStruct((rows // 2, features), bf),
        ],
        compiler_params=params,
        cost_estimate=pl.CostEstimate(
            flops=6 * rows * features * part,
            bytes_accessed=4 * features * part + 5 * rows * features + 14 * rows * part,
            transcendentals=rows * part,
        ),
        name="ffn_rows",
    )(n2, gate, d_hidden, w_gate, w_up)
    return n2, seed, hidden, d_gate, d_up, d_same, d_other


def ffn_sums(n2, seed, hid, dgate, dup, g_gate, g_up, g_down, turned):
    @pl.when(pl.program_id(0) == 0)
    def _():
        turned[...] = hid[...].T

    bf = jnp.bfloat16
    g_gate[...] = across(n2[...], dgate[...]).astype(bf)
    g_up[...] = across(n2[...], dup[...]).astype(bf)
    g_down[...] = dot(turned[...], seed[...]).astype(bf)


def weight_sums(n2, seed, hid, dgate, dup):
    rows, features = n2.shape
    part = hid.shape[1]
    tile = features // 4
    bf = jnp.bfloat16
    column = lambda height: pl.BlockSpec((height, tile), lambda i: (0, i))
    whole = pl.BlockSpec((rows, part), lambda i: (0, 0))
    return pl.pallas_call(
        ffn_sums,
        grid=(4,),
        in_specs=[column(rows), column(rows), whole, whole, whole],
        out_specs=[
            pl.BlockSpec((tile, part), lambda i: (i, 0)),
            pl.BlockSpec((tile, part), lambda i: (i, 0)),
            column(part),
        ],
        out_shape=[
            jax.ShapeDtypeStruct((features, part), bf),
            jax.ShapeDtypeStruct((features, part), bf),
            jax.ShapeDtypeStruct((part, features), bf),
        ],
        scratch_shapes=[pltpu.VMEM((part, rows), bf)],
        compiler_params=pltpu.CompilerParams(vmem_limit_bytes=48 * 2**20),
        cost_estimate=pl.CostEstimate(
            flops=6 * rows * features * part,
            bytes_accessed=4 * rows * features + 6 * rows * part + 6 * features * part,
            transcendentals=0,
        ),
        name="ffn_sums",
    )(n2, seed, hid, dgate, dup)


def reduce_rows(same, other, beside=(), after=()):
    count = lax.axis_size("near") * lax.axis_size("ctx")
    arrived = mate(other.astype(jnp.bfloat16), 1)
    arrived, *after = lax.optimization_barrier((arrived, *after))
    total = same + arrived.astype(jnp.float32)
    blocks = total.reshape(count // 2, -1, total.shape[-1])
    sent = blocks.astype(jnp.bfloat16)
    result, *beside = lax.optimization_barrier((blocks[0], *beside))
    for k in range(1, count // 2):
        result = result + mate(sent[k], 2 * k).astype(jnp.float32)
    return (result, *beside, *after) if beside or after else result


def flipped(values):
    me = lax.axis_index("ctx")
    count = lax.axis_size("ctx")
    bit = 1
    while bit < count:
        v = values.reshape(values.shape[0], count // (2 * bit), 2, bit, *values.shape[2:])
        swapped = jnp.concatenate([v[:, :, 1:], v[:, :, :1]], axis=2)
        values = jnp.where((me & bit) != 0, swapped, v).reshape(values.shape)
        bit *= 2
    return values


def in_order(blocks):
    count = blocks.shape[0]
    me = lax.axis_index("near") * lax.axis_size("ctx") + lax.axis_index("ctx")
    bit = 1
    while bit < count:
        v = blocks.reshape(count // (2 * bit), 2, bit, *blocks.shape[1:])
        swapped = jnp.concatenate([v[:, 1:], v[:, :1]], axis=1)
        blocks = jnp.where((me & bit) != 0, swapped, v).reshape(blocks.shape)
        bit *= 2
    return blocks


def dot(a, b):
    return jnp.dot(a, b, preferred_element_type=jnp.float32)


def across(a, b):
    return lax.dot_general(a, b, (((0,), (0,)), ((), ())), preferred_element_type=jnp.float32)


def against(a, b):
    return lax.dot_general(a, b, (((1,), (1,)), ((), ())), preferred_element_type=jnp.float32)


def scale_rows(values):
    return lax.rsqrt(jnp.mean(values * values, axis=-1, keepdims=True) + EPS)


def norm_back(grad_normed, normed, inverse):
    return inverse * (grad_normed - normed * jnp.mean(grad_normed * normed, axis=-1, keepdims=True))


def on_device(
    tokens,
    segments,
    norm_gain,
    in_weight,
    conv_taps,
    out_weight,
    ffn_gain,
    gate_weight,
    up_weight,
    down_weight,
    cotangent,
):
    seq_count, seq_rows, features = tokens.shape
    rows = seq_count * seq_rows
    n_far = lax.axis_size("far")
    n_near = lax.axis_size("near")
    n_ctx = lax.axis_size("ctx")
    members = n_near * n_ctx
    own = in_weight.shape[0]
    own_ff = down_weight.shape[0]
    part = features // members
    part_ff = n_far * own_ff
    bf, f32 = jnp.bfloat16, jnp.float32
    gain_two = ffn_gain.astype(f32)[:, None]

    everyone = ("far",) + PLANE
    total = n_far * members
    own_tokens = tokens.reshape(rows, features)
    seed_rows = cotangent.reshape(rows, features)

    small = jnp.zeros((16, 128), bf)
    small = small.at[0, :own].set(norm_gain)
    small = small.at[8 : 8 + rows // 128, :].set(segments.reshape(rows // 128, 128).astype(bf))
    small = jnp.broadcast_to(small[None], (total, 16, 128))
    small = lax.all_to_all(small, everyone, split_axis=0, concat_axis=0, tiled=True)
    gain_row = small[:, 0, :own].reshape(features).astype(f32)
    seg_all = lax.dynamic_slice_in_dim(small, lax.axis_index("far") * members, members, axis=0)
    seg_all = seg_all[:, 8 : 8 + rows // 128].reshape(members, rows)
    in_cut = in_weight.reshape(own, 3, total, own).transpose(2, 0, 1, 3)
    in_cut = in_cut.reshape(n_far, members, own, 3, own).transpose(1, 2, 3, 0, 4)
    in_cut = in_cut.reshape(1, members, own, 3 * part)
    in_cut = jnp.broadcast_to(in_cut, (n_far, members, own, 3 * part))
    in_cut = in_cut.reshape(total, own, 3 * part)
    in_cut = lax.all_to_all(in_cut, everyone, split_axis=0, concat_axis=0, tiled=True)
    w_in = in_cut.reshape(features, 3 * part)
    tap_rows = jnp.pad(conv_taps, ((0, 13), (0, features - own)))
    lower = jnp.concatenate([down_weight, out_weight, tap_rows], axis=0)
    lower = lax.all_gather(lower, "far", axis=0, tiled=False)
    w_down = lower[:, :own_ff].reshape(part_ff, features)
    w_out = lower[:, own_ff : own_ff + own].reshape(part, features)
    taps = lower[:, own_ff + own : own_ff + own + 3, :own].astype(f32)
    taps = taps.transpose(1, 0, 2).reshape(3, part)

    def cut_ff(weight):
        scaled = (weight.astype(f32) * gain_two).astype(bf)
        cut = scaled.reshape(own, n_far, members, own_ff).transpose(2, 0, 1, 3)
        return cut.reshape(members, own, part_ff)

    gu_cut = jnp.stack([cut_ff(gate_weight), cut_ff(up_weight)], axis=1)
    gu_cut = lax.all_to_all(gu_cut, PLANE, split_axis=0, concat_axis=0, tiled=True)
    w_gate = lax.all_gather(
        gu_cut[:, 0].reshape(members * own, part_ff), "far", axis=0, tiled=True
    )
    w_up = lax.all_gather(gu_cut[:, 1].reshape(members * own, part_ff), "far", axis=0, tiled=True)

    seg_true = seg_all.reshape(n_near, n_ctx, seq_count, seq_rows).transpose(0, 2, 1, 3)
    me_near = lax.axis_index("near")
    seg_true = jnp.where(me_near == 0, seg_true, seg_true[::-1])
    length = n_ctx * seq_rows
    seg_true = seg_true.reshape(n_near * seq_count, length)
    outside = jnp.full((n_near * seq_count, 2), -1, bf)
    seg_ext = jnp.concatenate([outside, seg_true], axis=1)
    keep1 = (seg_ext[:, 1 : length + 1] == seg_true).astype(f32)[:, :, None]
    keep2 = (seg_ext[:, :length] == seg_true).astype(f32)[:, :, None]

    def to_true(same, other):
        v = jnp.stack(
            [
                same.reshape(n_near, n_ctx // 2, seq_count, seq_rows, -1),
                other.reshape(n_near, n_ctx // 2, seq_count, seq_rows, -1),
            ],
            axis=2,
        )
        v = flipped(v.reshape(n_near, n_ctx, seq_count, seq_rows, -1))
        return v.transpose(0, 2, 1, 3, 4).reshape(n_near * seq_count, length, -1)

    def to_relative(v):
        v = v.reshape(n_near, seq_count, n_ctx, seq_rows, -1).transpose(0, 2, 1, 3, 4)
        v = flipped(v).reshape(n_near, n_ctx // 2, 2, seq_count, seq_rows, -1)
        half = members // 2 * rows
        return v[:, :, 0].reshape(half, -1), v[:, :, 1].reshape(half, -1)

    def shifted(v, steps):
        fill = jnp.zeros((v.shape[0], abs(steps), v.shape[2]), v.dtype)
        if steps > 0:
            return jnp.concatenate([fill, v[:, :-steps]], axis=1)
        return jnp.concatenate([v[:, -steps:], fill], axis=1)

    def normalized(t):
        v = t.astype(f32)
        return (v * scale_rows(v) * gain_row).astype(bf)

    def summed(left, right):
        return across(left[0], right[0]) + across(left[1], right[1])

    x_all = collect(own_tokens)
    x_all, seed_rows = lax.optimization_barrier((x_all, seed_rows))
    seed_all = collect(seed_rows)
    w_in, seed_all = lax.optimization_barrier((w_in, seed_all))
    x_all = halves(x_all)
    h_in = tuple(normalized(t) for t in x_all)
    proj = [dot(n, w_in) for n in h_in]
    part_b = [p[:, :part] for p in proj]
    part_c = [p[:, part : 2 * part] for p in proj]
    part_x = [p[:, 2 * part :] for p in proj]
    mixed_in = to_true(*[(b * x).astype(bf) for b, x in zip(part_b, part_x)]).astype(f32)
    previous = shifted(mixed_in, 1) * keep1
    earlier = shifted(mixed_in, 2) * keep2
    short = to_relative(taps[2] * mixed_in + taps[1] * previous + taps[0] * earlier)
    gated = [(c * s).astype(bf) for c, s in zip(part_c, short)]
    branch = reduce_rows(*[dot(g, w_out) for g in gated])
    resid = own_tokens.astype(f32) + branch
    inverse2 = scale_rows(resid)
    normed2 = resid * inverse2

    n2_all = collect(normed2.astype(bf))
    n2_all, seed_all, hidden, d_gate, d_up, d_same, d_other = ffn(
        n2_all, seed_all, w_gate, w_up, w_down
    )
    sum_gate, sum_up, sum_down = weight_sums(n2_all, seed_all, hidden, d_gate, d_up)
    sum_down = sum_down.reshape(n_far, own_ff, features)
    d_n2, sum_gate, sum_up, sum_down = reduce_rows(
        d_same, d_other, beside=(sum_gate, sum_up, sum_down)
    )
    own_gu = jnp.stack(
        [
            lax.psum_scatter(sum_gate, "far", scatter_dimension=0, tiled=True),
            lax.psum_scatter(sum_up, "far", scatter_dimension=0, tiled=True),
        ]
    )
    d_resid = seed_rows.astype(f32) + norm_back(d_n2, normed2, inverse2)

    d_branch = collect(d_resid.astype(bf))
    d_branch = halves(d_branch)
    d_branch, hidden = lax.optimization_barrier((d_branch, hidden))
    mixed = resid + reduce_rows(*[dot(h, w_down) for h in jnp.split(hidden, 2)])
    mixed = mixed.astype(bf)
    d_gated = [against(d, w_out) for d in d_branch]
    d_short = to_true(*[(d * c).astype(bf) for d, c in zip(d_gated, part_c)]).astype(f32)
    sum_taps = jnp.stack(
        [
            jnp.sum(d_short * earlier, axis=(0, 1)),
            jnp.sum(d_short * previous, axis=(0, 1)),
            jnp.sum(d_short * mixed_in, axis=(0, 1)),
        ]
    )
    d_mixed = to_relative(
        taps[2] * d_short
        + shifted(taps[1] * keep1 * d_short, -1)
        + shifted(taps[0] * keep2 * d_short, -2)
    )
    d_proj = [
        jnp.concatenate([dm * x, dg * s, dm * b], axis=1).astype(bf)
        for dm, dg, s, b, x in zip(d_mixed, d_gated, short, part_b, part_x)
    ]
    sum_in = summed(h_in, d_proj).astype(bf).reshape(total, own, 3 * part)
    d_proj, sum_in = lax.optimization_barrier((d_proj, sum_in))
    d_n1 = reduce_rows(*[against(d, w_in) for d in d_proj]) * gain_row
    values = own_tokens.astype(f32)
    inverse1 = scale_rows(values)
    input_grad = d_resid + norm_back(d_n1, values * inverse1, inverse1)

    own_in = lax.all_to_all(sum_in, everyone, split_axis=0, concat_axis=0, tiled=True)
    own_in = own_in.reshape(n_far, members, own, 3 * part).astype(f32).sum(axis=0)
    own_in = own_in.reshape(members, own, 3, n_far, own).transpose(1, 2, 3, 0, 4)
    grad_in = own_in.reshape(own, 3 * features)
    grad_gain1 = jnp.sum(in_weight.astype(f32) * grad_in, axis=1) / norm_gain.astype(f32)
    sum_out = summed(gated, d_branch).astype(bf).reshape(n_far, own, features)
    tap_sums = sum_taps.astype(bf).reshape(3, n_far, own).transpose(1, 0, 2)
    tap_sums = jnp.pad(tap_sums, ((0, 0), (0, 13), (0, features - own)))
    lower_sum = jnp.concatenate([sum_down, sum_out, tap_sums], axis=1)
    own_gu = own_gu.reshape(2, members, own, part_ff).transpose(1, 0, 2, 3)
    own_gu = lax.all_to_all(own_gu, PLANE, split_axis=0, concat_axis=0, tiled=True)
    own_lower = lax.psum_scatter(lower_sum, "far", scatter_dimension=0, tiled=False)
    own_lower = own_lower.astype(f32)
    grad_out = own_lower[own_ff : own_ff + own]
    grad_taps = own_lower[own_ff + own : own_ff + own + 3, :own]
    own_gu = own_gu.reshape(members, 2, own, n_far, own_ff).transpose(1, 2, 3, 0, 4)
    own_gu = own_gu.reshape(2, own, members * part_ff).astype(f32)
    grad_gate = own_gu[0] * gain_two
    grad_up = own_gu[1] * gain_two
    grad_gain2 = jnp.sum(
        gate_weight.astype(f32) * own_gu[0] + up_weight.astype(f32) * own_gu[1], axis=1
    )
    return (
        mixed.reshape(seq_count, seq_rows, features),
        input_grad.reshape(seq_count, seq_rows, features),
        grad_gain1,
        grad_in,
        grad_taps,
        grad_out,
        grad_gain2,
        grad_gate,
        grad_up,
        own_lower[:own_ff],
    )


def solution(mesh):
    dp, ctx = mesh.shape["dp"], mesh.shape["ctx"]
    near = 2 if dp % 2 == 0 else 1
    fine = Mesh(mesh.devices.reshape(dp // near, near, ctx), ("far", "near", "ctx"))
    seq = ("far", "near")
    every = ("far", "near", "ctx")
    in_specs = (
        P(seq, "ctx", None),
        P(seq, "ctx"),
        P(every),
        P(every, None),
        P(None, every),
        P(every, None),
        P(every),
        P(every, None),
        P(every, None),
        P(every, None),
        P(seq, "ctx", None),
    )
    out_specs = (
        P(seq, "ctx", None),
        P(seq, "ctx", None),
        P(every),
        P(every, None),
        P(None, every),
        P(every, None),
        P(every),
        P(every, None),
        P(every, None),
        P(every, None),
    )
    return jax.shard_map(
        on_device, mesh=fine, in_specs=in_specs, out_specs=out_specs, check_vma=False
    )
```
